32 devices in a mesh: dom: 16 (over z, y, x), level: 2 (over core).
Axes of the slice: x: 2, y: 2, z: 4, core: 2. Of those that a mesh axis runs over, the one named last changes fastest.
Arguments:
- residual: float32 [1024, 32, 256], P(('dom', 'level')), may hold values from -6 to 6
- neighbours: int32 [1024, 2], P(('dom', 'level')), may hold values from 0 to 1023, as said below
- pattern: int32 [1024, 6], P(('dom', 'level')), may hold values 0 or 1
- diag_inverse: bfloat16 [1024, 4, 4096], P(('dom', 'level')), may hold values from -2.5 to 2.5
- lower_blocks: bfloat16 [1024, 6, 4096], P(('dom', 'level')), may hold values from -0.44921875 to 0.44921875
- phi: bfloat16 [1024, 192, 256], P(('dom', 'level')), may hold values from -0.375 to 0.375
- aggregate: int32 [1024], P(('dom', 'level')), may hold values from 0 to 127, as said below
- level1_restrict: bfloat16 [196608, 192], P(('dom', 'level')), may hold values from -0.4375 to 0.4375
- level2_interior_solve: bfloat16 [24576, 192], P(('dom', 'level')), may hold values from -1 to 1
- level2_restrict: bfloat16 [24576, 192], P(('dom', 'level')), may hold values from -0.4375 to 0.4375
- level3_interior_solve: bfloat16 [3072, 192], P('dom'), may hold values from -1 to 1
- level3_restrict: bfloat16 [3072, 192], P('dom'), may hold values from -0.4375 to 0.4375
- level4_interior_solve: bfloat16 [384, 192], replicated, may hold values from -1 to 1
- level4_restrict: bfloat16 [384, 192], replicated, may hold values from -0.4375 to 0.4375
- top_inverse: bfloat16 [192, 192], replicated, may hold values from -1 to 1
Outputs:
- correction: float32 [1024, 32, 256], P(('dom', 'level'))
The draws below stay inside these ranges and needn't reach their ends.
Inputs may be any that keep to these rules, and one draw needn't show every extreme that they name: Subdomains come in blocks of 32 consecutive ones. neighbours[s, 0] lies in the block before s's own (in s's own block for the first block) and neighbours[s, 1] in the block after (in s's own block for the last); each column names every subdomain of such a target block exactly once from the block that points at it. Every aggregate holds exactly 8 subdomains of one block of 32 consecutive subdomains; block b holds the aggregates b * 4 to (b + 1) * 4 - 1.
All inputs are finite; a program needn't handle non-finite values. No bound on the sum of `pattern` on one device may be relied on, other than what follows from the above.
Results may differ from the reference program's by a relative error of at most 0.0003.
Values sent between devices are 32-bit elements; how exact they have to be, the bound alone decides.
A program may use at most 128 MiB of HBM per device.

```python
import jax
import jax.numpy as jnp
from jax import lax

BS = 64
NB = 4
NI = 256
COARSE_WIDTH = 192
SUB_DEV = 32
NRHS = 32
SUBS = 1024
AGGREGATE_COUNT = 128
LEVEL4_GROUPS = 2
NPAIR = 6
N_DOM = 16


def block_orders(key):
    block_total = SUBS // SUB_DEV
    base_order = jnp.tile(jnp.arange(SUB_DEV, dtype=jnp.int32)[None, :], (block_total, 1))
    return jax.random.permutation(key, base_order, axis=1, independent=True)


def draw_neighbours(key, part):
    block_total = SUBS // SUB_DEV
    subkeys = jax.random.split(jax.random.fold_in(key, 11), 2)
    before_perm = block_orders(subkeys[0])
    after_perm = block_orders(subkeys[1])
    block_ids = jnp.arange(block_total, dtype=jnp.int32)[:, None]
    before_ids = jnp.maximum(block_ids - 1, 0) * SUB_DEV + before_perm
    after_ids = jnp.minimum(block_ids + 1, block_total - 1) * SUB_DEV + after_perm
    return jnp.stack([before_ids.reshape(-1), after_ids.reshape(-1)], axis=1).astype(jnp.int32)


def draw_aggregate(key, part):
    block_total = SUBS // SUB_DEV
    orders = block_orders(jax.random.fold_in(key, 23))
    block_ids = jnp.arange(block_total, dtype=jnp.int32)[:, None]
    owners = block_ids * (SUB_DEV // 8) + orders // 8
    return owners.reshape(-1).astype(jnp.int32)


def dominant_values(key, is_diag, size, scale):
    subkeys = jax.random.split(key, 2)
    shape = is_diag.shape
    diag_part = jnp.exp(jax.random.uniform(subkeys[0], shape, jnp.float32, jnp.log(0.5), jnp.log(2.0)))
    off_part = jax.random.truncated_normal(subkeys[1], -3.0, 3.0, shape, jnp.float32) * 0.3 / math_sqrt(size)
    return (scale * jnp.where(is_diag, diag_part, off_part)).astype(jnp.bfloat16)


def math_sqrt(number):
    return float(number) ** 0.5


def coarse_matrix(key, row_count, scale):
    row_ids = lax.broadcasted_iota(jnp.int32, (row_count, COARSE_WIDTH), 0)
    col_ids = lax.broadcasted_iota(jnp.int32, (row_count, COARSE_WIDTH), 1)
    return dominant_values(key, row_ids % COARSE_WIDTH == col_ids, COARSE_WIDTH, scale)


def draw_diag_inverse(key, part):
    flat_ids = lax.broadcasted_iota(jnp.int32, (SUBS, NB, BS * BS), 2)
    return dominant_values(jax.random.fold_in(key, 31), flat_ids % (BS + 1) == 0, BS, 1.0)


def draw_level2_interior_solve(key, part):
    return coarse_matrix(jax.random.fold_in(key, 41), AGGREGATE_COUNT * COARSE_WIDTH, 8.0 ** (-0.5))


def draw_level3_interior_solve(key, part):
    return coarse_matrix(jax.random.fold_in(key, 43), N_DOM * COARSE_WIDTH, 8.0 ** (-1.0))


def draw_level4_interior_solve(key, part):
    return coarse_matrix(jax.random.fold_in(key, 47), LEVEL4_GROUPS * COARSE_WIDTH, 8.0 ** (-1.5))


def draw_top_inverse(key, part):
    return coarse_matrix(jax.random.fold_in(key, 53), COARSE_WIDTH, 8.0 ** (-1.5) * float(LEVEL4_GROUPS) ** (-0.5))


def plant(array, key, low, top_value):
    longest = array.shape.index(max(array.shape))
    spots = []
    for shift in (0, 1):
        where = [jax.random.randint(jax.random.fold_in(key, axis), (), 0, length) for axis, length in enumerate(array.shape)]
        where[longest] = (where[longest] + shift) % array.shape[longest]
        spots.append(tuple(where))
    return array.at[spots[0]].set(low).at[spots[1]].set(top_value)


def shard_levels(key, extent, cuts, smallest, top_value):
    def one(position, blocks):
        steps = jax.random.uniform(jax.random.fold_in(jax.random.fold_in(key, 6), position), (blocks,), jnp.float32, smallest / len(cuts), top_value / len(cuts))
        return jnp.repeat(jnp.exp(steps), extent[position] // blocks).reshape((-1,) + (1,) * (len(extent) - position - 1))

    loudness = one(*cuts[0])
    for cut in cuts[1:]:
        loudness = loudness * one(*cut)
    return loudness


def bell_draw(key, extent, spread, most, cuts=(), kind=jnp.bfloat16):
    values = spread * jax.random.normal(key, extent, jnp.float32)
    if cuts:
        values = values * shard_levels(key, extent, cuts, -0.22, 0.18)
    return jnp.clip(values, -most, most).astype(kind)


def setup_inputs(seed: int = 0) -> dict:
    streams_of = jax.random.split(jax.random.key(seed), 16)
    residual = bell_draw(streams_of[0], (SUBS, NRHS, NI), 1.0, 6.0, ((0, 32),), jnp.float32)
    neighbours = draw_neighbours(jax.random.fold_in(streams_of[15], 71), 0)
    pattern = plant((jax.random.randint(streams_of[2], (SUBS, NPAIR), 0, 3) < 2).astype(jnp.int32), jax.random.fold_in(streams_of[2], 1), 0, 1)
    diag_inverse = draw_diag_inverse(jax.random.fold_in(streams_of[15], 71), 0)
    lower_blocks = bell_draw(streams_of[4], (SUBS, NPAIR, BS * BS), 0.075, 0.44921875, ((0, 32),))
    phi = bell_draw(streams_of[5], (SUBS, COARSE_WIDTH, NI), NI ** -0.5, 0.375, ((0, 32),))
    aggregate = draw_aggregate(jax.random.fold_in(streams_of[15], 71), 0)
    level1_restrict = bell_draw(streams_of[7], (SUBS * COARSE_WIDTH, COARSE_WIDTH), COARSE_WIDTH ** -0.5, 0.4375, ((0, 32),))
    level2_interior_solve = draw_level2_interior_solve(jax.random.fold_in(streams_of[15], 71), 0)
    level2_restrict = bell_draw(streams_of[9], (AGGREGATE_COUNT * COARSE_WIDTH, COARSE_WIDTH), COARSE_WIDTH ** -0.5, 0.4375, ((0, 32),))
    level3_interior_solve = draw_level3_interior_solve(jax.random.fold_in(streams_of[15], 71), 0)
    level3_restrict = bell_draw(streams_of[11], (N_DOM * COARSE_WIDTH, COARSE_WIDTH), COARSE_WIDTH ** -0.5, 0.4375, ((0, 16),))
    level4_interior_solve = draw_level4_interior_solve(jax.random.fold_in(streams_of[15], 71), 0)
    level4_restrict = bell_draw(streams_of[13], (LEVEL4_GROUPS * COARSE_WIDTH, COARSE_WIDTH), COARSE_WIDTH ** -0.5, 0.4375)
    top_inverse = draw_top_inverse(jax.random.fold_in(streams_of[15], 71), 0)
    return dict(residual=residual, neighbours=neighbours, pattern=pattern, diag_inverse=diag_inverse, lower_blocks=lower_blocks, phi=phi, aggregate=aggregate, level1_restrict=level1_restrict, level2_interior_solve=level2_interior_solve, level2_restrict=level2_restrict, level3_interior_solve=level3_interior_solve, level3_restrict=level3_restrict, level4_interior_solve=level4_interior_solve, level4_restrict=level4_restrict, top_inverse=top_inverse)


FULL_ACCURACY = lax.Precision.HIGHEST


def pair_index(upper_block, lower_block):
    return upper_block * (upper_block - 1) // 2 + lower_block


def block_apply(blocks, vector, transpose):
    block_width = vector.shape[2]
    square = blocks.astype(jnp.float32).reshape(blocks.shape[0], block_width, block_width)
    if transpose:
        return jnp.einsum("sio,sri->sro", square, vector, precision=FULL_ACCURACY)
    return jnp.einsum("soi,sri->sro", square, vector, precision=FULL_ACCURACY)


def forward_block(sources, forward, block_id, pair_mask, lower_blocks):
    current = sources[block_id]
    for prior_id in range(block_id):
        pair_slot = pair_index(block_id, prior_id)
        current = current - pair_mask[:, pair_slot][:, None, None] * block_apply(lower_blocks[:, pair_slot], forward[prior_id], False)
    return current


def finish_solve(forward, pair_mask, diag_inverse, lower_blocks):
    block_count = len(forward)
    middle = [block_apply(diag_inverse[:, block_id], forward[block_id], False) for block_id in range(block_count)]
    result = [None] * block_count
    for block_id in reversed(range(block_count)):
        current = middle[block_id]
        for later_id in range(block_id + 1, block_count):
            pair_slot = pair_index(later_id, block_id)
            current = current - pair_mask[:, pair_slot][:, None, None] * block_apply(lower_blocks[:, pair_slot], result[later_id], True)
        result[block_id] = current
    return jnp.concatenate(result, axis=2)


def reference(residual, neighbours, pattern, diag_inverse, lower_blocks, phi, aggregate, level1_restrict, level2_interior_solve, level2_restrict, level3_interior_solve, level3_restrict, level4_interior_solve, level4_restrict, top_inverse):
    iface_dofs = 2 * BS
    edge_rows = residual[:, :, NI - iface_dofs:]
    assembled = (edge_rows + edge_rows[neighbours[:, 0]] + edge_rows[neighbours[:, 1]]) / 3.0
    assembled_rhs = jnp.concatenate([residual[:, :, :NI - iface_dofs], assembled], axis=2)
    pair_mask = pattern.astype(jnp.float32)
    block_total = SUBS // SUB_DEV

    def fine_part(block_index):
        first_row = block_index * SUB_DEV
        rhs_block = lax.dynamic_slice_in_dim(assembled_rhs, first_row, SUB_DEV, 0)
        mask_block = lax.dynamic_slice_in_dim(pair_mask, first_row, SUB_DEV, 0)
        diag_block = lax.dynamic_slice_in_dim(diag_inverse, first_row, SUB_DEV, 0)
        lower_part = lax.dynamic_slice_in_dim(lower_blocks, first_row, SUB_DEV, 0)
        phi_block = lax.dynamic_slice_in_dim(phi, first_row, SUB_DEV, 0).astype(jnp.float32)
        restrict_block = lax.dynamic_slice_in_dim(level1_restrict, first_row * COARSE_WIDTH, SUB_DEV * COARSE_WIDTH, 0).astype(jnp.float32).reshape(SUB_DEV, COARSE_WIDTH, COARSE_WIDTH)
        sources = [rhs_block[:, :, block_id * BS:(block_id + 1) * BS] for block_id in range(NB)]
        forward = []
        for block_id in range(NB):
            forward.append(forward_block(sources, forward, block_id, mask_block, lower_part))
        fine_x = finish_solve(forward, mask_block, diag_block, lower_part)
        coarse_rhs = jnp.einsum("ski,sri->srk", phi_block, rhs_block, precision=FULL_ACCURACY)
        level1_terms = jnp.einsum("sri,sij->srj", coarse_rhs, restrict_block, precision=FULL_ACCURACY)
        return fine_x, level1_terms

    block_ids = jnp.arange(block_total, dtype=jnp.int32)
    fine_all, terms_all = lax.map(fine_part, block_ids)
    fine_all = fine_all.reshape(SUBS, NRHS, NI)
    terms_all = terms_all.reshape(SUBS, NRHS, COARSE_WIDTH)
    level2_residual = jax.ops.segment_sum(terms_all, aggregate, num_segments=AGGREGATE_COUNT)
    level2_matrices = level2_restrict.astype(jnp.float32).reshape(AGGREGATE_COUNT, COARSE_WIDTH, COARSE_WIDTH)
    level2_eliminated = level2_interior_solve.astype(jnp.float32).reshape(AGGREGATE_COUNT, COARSE_WIDTH, COARSE_WIDTH)
    level2_terms = jnp.einsum("ari,aij->arj", level2_residual, level2_matrices, precision=FULL_ACCURACY)
    per_processor = AGGREGATE_COUNT // N_DOM
    level3_residual = level2_terms.reshape(N_DOM, per_processor, NRHS, COARSE_WIDTH).sum(axis=1)
    level3_matrices = level3_restrict.astype(jnp.float32).reshape(N_DOM, COARSE_WIDTH, COARSE_WIDTH)
    level3_eliminated = level3_interior_solve.astype(jnp.float32).reshape(N_DOM, COARSE_WIDTH, COARSE_WIDTH)
    level3_terms = jnp.einsum("cri,cij->crj", level3_residual, level3_matrices, precision=FULL_ACCURACY)
    level4_residual = level3_terms.reshape(LEVEL4_GROUPS, 8, NRHS, COARSE_WIDTH).sum(axis=1)
    level4_matrices = level4_restrict.astype(jnp.float32).reshape(LEVEL4_GROUPS, COARSE_WIDTH, COARSE_WIDTH)
    level4_eliminated = level4_interior_solve.astype(jnp.float32).reshape(LEVEL4_GROUPS, COARSE_WIDTH, COARSE_WIDTH)
    top_resid = jnp.einsum("pri,pij->rj", level4_residual, level4_matrices, precision=FULL_ACCURACY)
    top_correction = jnp.einsum("ik,rk->ri", top_inverse.astype(jnp.float32), top_resid, precision=FULL_ACCURACY)
    level4_correction = jnp.einsum("muh,mch->mcu", level4_eliminated, level4_residual, precision=FULL_ACCURACY) + jnp.einsum("bsv,lv->bls", level4_matrices, top_correction, precision=FULL_ACCURACY)
    level3_correction = jnp.einsum("hsj,hyj->hys", level3_eliminated, level3_residual, precision=FULL_ACCURACY) + jnp.einsum("lzb,lkb->lkz", level3_matrices, jnp.repeat(level4_correction, 8, axis=0), precision=FULL_ACCURACY)
    level2_correction = jnp.einsum("bpf,bxf->bxp", level2_eliminated, level2_residual, precision=FULL_ACCURACY) + jnp.einsum("knp,kep->ken", level2_matrices, jnp.repeat(level3_correction, per_processor, axis=0), precision=FULL_ACCURACY)

    def prolong_part(block_index):
        first_row = block_index * SUB_DEV
        phi_block = lax.dynamic_slice_in_dim(phi, first_row, SUB_DEV, 0).astype(jnp.float32)
        restrict_block = lax.dynamic_slice_in_dim(level1_restrict, first_row * COARSE_WIDTH, SUB_DEV * COARSE_WIDTH, 0).astype(jnp.float32).reshape(SUB_DEV, COARSE_WIDTH, COARSE_WIDTH)
        owners = lax.dynamic_slice_in_dim(aggregate, first_row, SUB_DEV, 0)
        fine_block = lax.dynamic_slice_in_dim(fine_all, first_row, SUB_DEV, 0)
        coarse_corr = jnp.einsum("sij,srj->sri", restrict_block, level2_correction[owners], precision=FULL_ACCURACY)
        return fine_block + jnp.einsum("ski,srk->sri", phi_block, coarse_corr, precision=FULL_ACCURACY)

    correction = lax.map(prolong_part, block_ids)
    return correction.reshape(SUBS, NRHS, NI)
```

```python
import functools

import jax
import jax.numpy as jnp
from jax import lax
from jax.experimental import pallas as pl
from jax.experimental.pallas import tpu as pltpu
from jax.sharding import PartitionSpec as P

MESH = pl.DeviceIdType.MESH
F32 = jnp.float32
BF16 = jnp.bfloat16
GROUP = 8
UNROLL = 4


def split(x):
    hi = x.astype(BF16)
    lo = (x - hi.astype(F32)).astype(BF16)
    return jnp.concatenate([hi, lo], axis=0)


def fold(y):
    half = y.shape[0] // 2
    return y[:half] + y[half:]


def mul(x, w):
    return fold(lax.dot_general(split(x), w, (((1,), (0,)), ((), ())), preferred_element_type=F32))


def mul_t(x, w):
    return fold(lax.dot_general(split(x), w, (((1,), (1,)), ((), ())), preferred_element_type=F32))


def near(ref, i):
    return ref[jnp.clip(i, 0, ref.shape[0] - 1)]


def kernel(
    n_dom,
    n_lev,
    neigh,
    pattern,
    agg,
    res_h,
    diag_h,
    lower_h,
    phi_h,
    l1_h,
    l2i_h,
    l2r_h,
    l3i_h,
    l3r_h,
    l4i_h,
    l4r_h,
    top_h,
    out_h,
    res,
    diag,
    lower,
    phi,
    l1,
    l2i,
    l2r,
    l3i,
    l3r,
    l4i,
    l4r,
    top,
    recv_l,
    recv_r,
    spread,
    wide,
    lmat,
    dmat,
    fine,
    l2res,
    l2corr,
    xsend,
    xrecv,
    totals,
    in_sem,
    halo_send,
    halo_recv,
    own_sem,
    x_send_sem,
    x_recv_sem,
    t_send_sem,
    t_recv_sem,
    out_sem,
):
    subs, rhs, dofs = res.shape
    npair = lower.shape[1]
    nblk = diag.shape[1]
    bs = dofs // nblk
    edge = 2 * bs
    inner = dofs - edge
    width = top.shape[0]
    n_agg = subs // 8
    n_groups = n_dom // GROUP
    tiles = lower.shape[2] // 128
    steps = subs // UNROLL

    dom = lax.axis_index("dom")
    lev = lax.axis_index("level")
    me = dom * n_lev + lev
    last = n_dom * n_lev - 1

    loads = []
    for i, (src, dst) in enumerate(
        [
            (lower_h, lower),
            (diag_h, diag),
            (res_h, res),
            (phi_h, phi),
            (l1_h, l1),
            (l2r_h, l2r),
            (l2i_h, l2i),
            (l3r_h, l3r),
            (l3i_h, l3i),
            (l4r_h, l4r),
            (l4i_h, l4i),
            (top_h, top),
        ]
    ):
        copy = pltpu.make_async_copy(src, dst, in_sem.at[i])
        copy.start()
        loads.append(copy)

    def at(d):
        return (d // n_lev, d % n_lev)

    partners = [(dom, lev + 1 - 2 * (lev % 2))]
    w = 1
    while w < GROUP:
        partners.append((dom + w - 2 * w * ((dom // w) % 2), lev))
        w *= 2
    others = [((dom + GROUP * k) % n_dom, lev) for k in range(1, n_groups)]
    back = [((dom + n_dom - GROUP * k) % n_dom, lev) for k in range(1, n_groups)]
    right = at(jnp.minimum(me + 1, last))
    left = at(jnp.maximum(me - 1, 0))

    barrier = pltpu.get_barrier_semaphore()
    for p in partners + others + back:
        pl.semaphore_signal(barrier, inc=1, device_id=p, device_id_type=MESH)

    @pl.when(me > 0)
    def _():
        pl.semaphore_signal(barrier, inc=1, device_id=left, device_id_type=MESH)

    @pl.when(me < last)
    def _():
        pl.semaphore_signal(barrier, inc=1, device_id=right, device_id_type=MESH)

    count = len(partners) + len(others) + len(back)

    @pl.when((me > 0) & (me < last))
    def _():
        pl.semaphore_wait(barrier, count + 2)

    @pl.when((me == 0) | (me == last))
    def _():
        pl.semaphore_wait(barrier, count + 1)

    edge_src = res_h.at[:, :, pl.ds(inner, edge)]
    to_right = pltpu.make_async_remote_copy(
        src_ref=edge_src,
        dst_ref=recv_l,
        send_sem=halo_send.at[0],
        recv_sem=halo_recv.at[0],
        device_id=right,
        device_id_type=MESH,
    )
    to_left = pltpu.make_async_remote_copy(
        src_ref=edge_src,
        dst_ref=recv_r,
        send_sem=halo_send.at[1],
        recv_sem=halo_recv.at[1],
        device_id=left,
        device_id_type=MESH,
    )
    own_l = pltpu.make_async_copy(edge_src, recv_l, own_sem.at[0])
    own_r = pltpu.make_async_copy(edge_src, recv_r, own_sem.at[1])

    @pl.when(me < last)
    def _():
        to_right.start()

    @pl.when(me == last)
    def _():
        own_r.start()

    @pl.when(me > 0)
    def _():
        to_left.start()

    @pl.when(me == 0)
    def _():
        own_l.start()

    loads[0].wait()
    loads[1].wait()
    wide[...] = jnp.zeros_like(wide)
    l2res[...] = jnp.zeros_like(l2res)
    low_lane = lax.broadcasted_iota(jnp.int32, (tiles, 128), 1) < bs

    def pair_rows(a, b):
        zero = jnp.zeros((tiles, 128), F32)
        a_even = zero if a is None else a
        b_even = zero if b is None else pltpu.roll(b, bs, 1)
        a_odd = zero if a is None else pltpu.roll(a, bs, 1)
        b_odd = zero if b is None else b
        return jnp.where(low_lane, a_even, b_even), jnp.where(low_lane, a_odd, b_odd)

    def unpack(s, carry):
        x = lower[s].astype(F32)
        y = diag[s].astype(F32)
        for t in range(tiles):
            spread[0, pl.ds(t * 8, npair), :] = x[:, t * 128 : (t + 1) * 128]
            spread[1, pl.ds(t * 8, nblk), :] = y[:, t * 128 : (t + 1) * 128]

        def block(kind, i):
            return spread[kind, pl.ds(i, tiles, stride=8), :]

        for b in range(nblk):
            for jp in range(nblk // 2):
                if 2 * jp < b:
                    parts = []
                    for j in (2 * jp, 2 * jp + 1):
                        if j < b:
                            slot = b * (b - 1) // 2 + j
                            parts.append(block(0, slot) * pattern[s, slot].astype(F32))
                        else:
                            parts.append(None)
                    even, odd = pair_rows(*parts)
                    wide[jp, pl.ds(b * bs, tiles, stride=2), :] = even
                    wide[jp, pl.ds(b * bs + 1, tiles, stride=2), :] = odd
            own = block(1, b)
            even, odd = pair_rows(*((own, None) if b % 2 == 0 else (None, own)))
            wide[nblk // 2, pl.ds(b * bs, tiles, stride=2), :] = even
            wide[nblk // 2, pl.ds(b * bs + 1, tiles, stride=2), :] = odd
        for jp in range(nblk // 2):
            lmat[s, :, pl.ds(jp * 128, 128)] = wide[jp].astype(BF16)
        dmat[s] = wide[nblk // 2].astype(BF16)
        return carry

    lax.fori_loop(0, subs, unpack, 0)

    for copy in loads[2:5]:
        copy.wait()

    @pl.when(me < last)
    def _():
        to_right.wait_send()
        to_left.wait_recv()

    @pl.when(me == last)
    def _():
        own_r.wait()

    @pl.when(me > 0)
    def _():
        to_left.wait_send()
        to_right.wait_recv()

    @pl.when(me == 0)
    def _():
        own_l.wait()

    base_l = jnp.maximum(me - 1, 0) * subs
    base_r = jnp.minimum(me + 1, last) * subs
    agg_base = me * n_agg

    def up(g, carry):
        ids = [g * UNROLL + u for u in range(UNROLL)]
        full = []
        for s in ids:
            mine = res[s]
            total = mine[:, inner:] + near(recv_l, neigh[s, 0] - base_l) + near(recv_r, neigh[s, 1] - base_r)
            full.append(jnp.concatenate([mine[:, :inner], total / 3.0], axis=1))
        for s, x in zip(ids, full):
            res[s] = x
        coarse = [mul_t(x, phi[s]) for s, x in zip(ids, full)]
        terms = [
            mul(x, l1[pl.ds(pl.multiple_of(s * width, width), width), :])
            for s, x in zip(ids, coarse)
        ]
        for a in range(n_agg):
            acc = l2res[a]
            for s, x in zip(ids, terms):
                acc = acc + jnp.where(agg[s] - agg_base == a, 1.0, 0.0).astype(F32) * x
            l2res[a] = acc
        return carry

    lax.fori_loop(0, steps, up, 0)

    for copy in loads[5:]:
        copy.wait()

    def fine_step(g, carry):
        ids = [g * UNROLL + u for u in range(UNROLL)]
        base = [res[s] for s in ids]
        x = base
        for _ in range(nblk - 1):
            x = [b - mul_t(v, lmat[s]) for s, b, v in zip(ids, base, x)]
        mid = []
        for s, v in zip(ids, x):
            cols = [
                mul_t(v[:, jp * 128 : (jp + 1) * 128], dmat[s, pl.ds(jp * 128, 128), :])
                for jp in range(nblk // 2)
            ]
            mid.append(jnp.concatenate(cols, axis=1))
        x = mid
        for _ in range(nblk - 1):
            x = [b - mul(v, lmat[s]) for s, b, v in zip(ids, mid, x)]
        for s, v in zip(ids, x):
            fine[s] = v
        return carry

    def exchange(i, value):
        xsend[i] = value
        copy = pltpu.make_async_remote_copy(
            src_ref=xsend.at[i],
            dst_ref=xrecv.at[i],
            send_sem=x_send_sem.at[i],
            recv_sem=x_recv_sem.at[i],
            device_id=partners[i],
            device_id_type=MESH,
        )
        copy.start()
        return copy

    n_gap = len(partners) + 1
    cuts = [steps * i // n_gap for i in range(n_gap + 1)]

    def work(i):
        lax.fori_loop(cuts[i], cuts[i + 1], fine_step, 0)

    part = mul(l2res[0], l2r[pl.ds(0, width), :])
    for a in range(1, n_agg):
        part = part + mul(l2res[a], l2r[pl.ds(a * width, width), :])
    copy = exchange(0, part)
    work(0)
    copy.wait()
    l3res = xsend[0] + xrecv[0]
    value = mul(l3res, l3r[...])
    for i in range(1, len(partners)):
        copy = exchange(i, value)
        work(i)
        copy.wait()
        value = xsend[i] + xrecv[i]
    group = dom // GROUP
    totals[group] = value
    sends = []
    for k in range(1, n_groups):
        copy = pltpu.make_async_remote_copy(
            src_ref=totals.at[group],
            dst_ref=totals.at[group],
            send_sem=t_send_sem.at[k - 1],
            recv_sem=t_recv_sem.at[k - 1],
            device_id=others[k - 1],
            device_id_type=MESH,
        )
        copy.start()
        sends.append(copy)
    work(n_gap - 1)
    for copy in sends:
        copy.wait()

    top_res = mul(totals[0], l4r[pl.ds(0, width), :])
    for p in range(1, n_groups):
        top_res = top_res + mul(totals[p], l4r[pl.ds(p * width, width), :])
    top_corr = mul_t(top_res, top[...])
    at_group = pl.ds(pl.multiple_of(group * width, width), width)
    l4corr = mul_t(totals[group], l4i[at_group, :]) + mul_t(top_corr, l4r[at_group, :])
    l3corr = mul_t(xsend[0] + xrecv[0], l3i[...]) + mul_t(l4corr, l3r[...])
    for a in range(n_agg):
        rows = pl.ds(a * width, width)
        l2corr[a] = mul_t(l2res[a], l2i[rows, :]) + mul_t(l3corr, l2r[rows, :])

    def down(g, carry):
        ids = [g * UNROLL + u for u in range(UNROLL)]
        q = [near(l2corr, agg[s] - agg_base) for s in ids]
        coarse = [
            mul_t(x, l1[pl.ds(pl.multiple_of(s * width, width), width), :]) for s, x in zip(ids, q)
        ]
        both = [mul(x, phi[s]) for s, x in zip(ids, coarse)]
        for s, x in zip(ids, both):
            fine[s] = fine[s] + x
        rows = pl.ds(g * UNROLL, UNROLL)
        pltpu.make_async_copy(fine.at[rows], out_h.at[rows], out_sem.at[g]).start()
        return carry

    lax.fori_loop(0, steps, down, 0)

    def drain(g, carry):
        rows = pl.ds(g * UNROLL, UNROLL)
        pltpu.make_async_copy(fine.at[rows], out_h.at[rows], out_sem.at[g]).wait()
        return carry

    lax.fori_loop(0, steps, drain, 0)


def solution(mesh):
    n_dom, n_lev = mesh.shape["dom"], mesh.shape["level"]

    def per_device(
        residual,
        neighbours,
        pattern,
        diag_inverse,
        lower_blocks,
        phi,
        aggregate,
        level1_restrict,
        level2_interior_solve,
        level2_restrict,
        level3_interior_solve,
        level3_restrict,
        level4_interior_solve,
        level4_restrict,
        top_inverse,
    ):
        subs, rhs, dofs = residual.shape
        width = top_inverse.shape[0]
        nblk = diag_inverse.shape[1]
        edge = 2 * (dofs // nblk)
        tiles = lower_blocks.shape[2] // 128
        n_agg = subs // 8
        n_groups = n_dom // GROUP
        n_x = 4
        large = [
            residual,
            diag_inverse,
            lower_blocks,
            phi,
            level1_restrict,
            level2_interior_solve,
            level2_restrict,
            level3_interior_solve,
            level3_restrict,
            level4_interior_solve,
            level4_restrict,
            top_inverse,
        ]
        scratch = [pltpu.VMEM(a.shape, a.dtype) for a in large]
        scratch += [
            pltpu.VMEM((subs, rhs, edge), F32),
            pltpu.VMEM((subs, rhs, edge), F32),
            pltpu.VMEM((2, tiles * 8, 128), F32),
            pltpu.VMEM((nblk // 2 + 1, dofs, 128), F32),
            pltpu.VMEM((subs, dofs, dofs), BF16),
            pltpu.VMEM((subs, dofs, 128), BF16),
            pltpu.VMEM((subs, rhs, dofs), F32),
            pltpu.VMEM((n_agg, rhs, width), F32),
            pltpu.VMEM((n_agg, rhs, width), F32),
            pltpu.VMEM((n_x, rhs, width), F32),
            pltpu.VMEM((n_x, rhs, width), F32),
            pltpu.VMEM((n_groups, rhs, width), F32),
            pltpu.SemaphoreType.DMA((len(large),)),
            pltpu.SemaphoreType.DMA((2,)),
            pltpu.SemaphoreType.DMA((2,)),
            pltpu.SemaphoreType.DMA((2,)),
            pltpu.SemaphoreType.DMA((n_x,)),
            pltpu.SemaphoreType.DMA((n_x,)),
            pltpu.SemaphoreType.DMA((max(n_groups - 1, 1),)),
            pltpu.SemaphoreType.DMA((max(n_groups - 1, 1),)),
            pltpu.SemaphoreType.DMA((subs // UNROLL,)),
        ]
        return pl.pallas_call(
            functools.partial(kernel, n_dom, n_lev),
            out_shape=jax.ShapeDtypeStruct(residual.shape, F32),
            in_specs=[pl.BlockSpec(memory_space=pltpu.SMEM)] * 3
            + [pl.BlockSpec(memory_space=pl.ANY)] * len(large),
            out_specs=pl.BlockSpec(memory_space=pl.ANY),
            scratch_shapes=scratch,
            compiler_params=pltpu.CompilerParams(
                collective_id=0, has_side_effects=True, vmem_limit_bytes=56 * 2**20
            ),
            cost_estimate=pl.CostEstimate(
                flops=10**9, bytes_accessed=13 * 10**6, transcendentals=0
            ),
        )(neighbours, pattern, aggregate, *large)

    both = P(("dom", "level"))
    in_specs = (both,) * 10 + (P("dom"),) * 2 + (P(),) * 3
    return jax.shard_map(
        per_device, mesh=mesh, in_specs=in_specs, out_specs=both, check_vma=False
    )
```

```python
import functools

import jax
import jax.numpy as jnp
from jax import lax
from jax.experimental import pallas as pl
from jax.experimental.pallas import tpu as pltpu
from jax.sharding import PartitionSpec as P

MESH = pl.DeviceIdType.MESH
F32 = jnp.float32
BF16 = jnp.bfloat16
GROUP = 8
UNROLL = 8
CHUNK = 16


def split(x):
    hi = x.astype(BF16)
    lo = (x - hi.astype(F32)).astype(BF16)
    return jnp.concatenate([hi, lo], axis=0)


def fold(y):
    half = y.shape[0] // 2
    return y[:half] + y[half:]


def mul(x, w):
    return fold(lax.dot_general(split(x), w, (((1,), (0,)), ((), ())), preferred_element_type=F32))


def mul_t(x, w):
    return fold(lax.dot_general(split(x), w, (((1,), (1,)), ((), ())), preferred_element_type=F32))


def window(size, index):
    low = index * size // 128 * 128
    return low, -(-((index + 1) * size) // 128) * 128, index * size - low


def mul_part(x, wt, off):
    pad = []
    if off:
        pad.append(jnp.zeros((x.shape[0], off), F32))
    pad.append(x)
    rest = wt.shape[1] - off - x.shape[1]
    if rest:
        pad.append(jnp.zeros((x.shape[0], rest), F32))
    return mul_t(jnp.concatenate(pad, axis=1) if len(pad) > 1 else x, wt)


def mul_part_t(x, wt, off, size):
    return mul(x, wt)[:, off : off + size]


def near(ref, i):
    return ref[jnp.clip(i, 0, ref.shape[0] - 1)]


def kernel(
    n_dom,
    n_lev,
    neigh,
    pattern,
    agg,
    res_h,
    diag_h,
    lower_h,
    phi_h,
    l1_h,
    l2i_h,
    l2r_h,
    l3i_h,
    l3r_h,
    l4i_h,
    l4r_h,
    top_h,
    out_h,
    res,
    diag,
    lower,
    phi,
    l1,
    l2i,
    l2r,
    l3i,
    l3r,
    l4i,
    l4r,
    top,
    recv_l,
    recv_r,
    spread,
    spread_d,
    wide,
    lmat,
    dmat,
    fine,
    l2res,
    l2corr,
    xsend,
    xrecv,
    totals,
    in_sem,
    halo_send,
    halo_recv,
    own_sem,
    x_send_sem,
    x_recv_sem,
    t_send_sem,
    t_recv_sem,
    out_sem,
):
    subs, rhs, dofs = res.shape
    npair = lower.shape[0]
    nblk = diag.shape[1]
    bs = dofs // nblk
    edge = 2 * bs
    inner = dofs - edge
    width = top.shape[0]
    n_agg = subs // 8
    n_groups = n_dom // GROUP
    tiles = lower.shape[2] // 128
    steps = subs // UNROLL

    dom = lax.axis_index("dom")
    lev = lax.axis_index("level")
    me = dom * n_lev + lev
    last = n_dom * n_lev - 1

    loads = []
    for i, (src, dst) in enumerate(
        [
            (lower_h, lower),
            (diag_h, diag),
            (res_h, res),
            (phi_h, phi),
            (l1_h, l1),
            (l2r_h, l2r),
            (l2i_h, l2i),
            (l3r_h, l3r),
            (l3i_h, l3i),
            (l4r_h, l4r),
            (l4i_h, l4i),
            (top_h, top),
        ]
    ):
        copy = pltpu.make_async_copy(src, dst, in_sem.at[i])
        copy.start()
        loads.append(copy)

    def at(d):
        return (d // n_lev, d % n_lev)

    partners = [(dom, lev + 1 - 2 * (lev % 2))]
    w = 1
    while w < GROUP:
        partners.append((dom + w - 2 * w * ((dom // w) % 2), lev))
        w *= 2
    others = [((dom + GROUP * k) % n_dom, lev) for k in range(1, n_groups)]
    back = [((dom + n_dom - GROUP * k) % n_dom, lev) for k in range(1, n_groups)]
    right = at(jnp.minimum(me + 1, last))
    left = at(jnp.maximum(me - 1, 0))

    barrier = pltpu.get_barrier_semaphore()
    for p in partners + others + back:
        pl.semaphore_signal(barrier, inc=1, device_id=p, device_id_type=MESH)

    @pl.when(me > 0)
    def _():
        pl.semaphore_signal(barrier, inc=1, device_id=left, device_id_type=MESH)

    @pl.when(me < last)
    def _():
        pl.semaphore_signal(barrier, inc=1, device_id=right, device_id_type=MESH)

    count = len(partners) + len(others) + len(back)

    @pl.when((me > 0) & (me < last))
    def _():
        pl.semaphore_wait(barrier, count + 2)

    @pl.when((me == 0) | (me == last))
    def _():
        pl.semaphore_wait(barrier, count + 1)

    edge_src = res_h.at[:, :, pl.ds(inner, edge)]
    to_right = pltpu.make_async_remote_copy(
        src_ref=edge_src,
        dst_ref=recv_l,
        send_sem=halo_send.at[0],
        recv_sem=halo_recv.at[0],
        device_id=right,
        device_id_type=MESH,
    )
    to_left = pltpu.make_async_remote_copy(
        src_ref=edge_src,
        dst_ref=recv_r,
        send_sem=halo_send.at[1],
        recv_sem=halo_recv.at[1],
        device_id=left,
        device_id_type=MESH,
    )
    own_l = pltpu.make_async_copy(edge_src, recv_l, own_sem.at[0])
    own_r = pltpu.make_async_copy(edge_src, recv_r, own_sem.at[1])

    @pl.when(me < last)
    def _():
        to_right.start()

    @pl.when(me == last)
    def _():
        own_r.start()

    @pl.when(me > 0)
    def _():
        to_left.start()

    @pl.when(me == 0)
    def _():
        own_l.start()

    loads[0].wait()
    loads[1].wait()
    wide[...] = jnp.zeros_like(wide)
    l2res[...] = jnp.zeros_like(l2res)
    low_lane = lax.broadcasted_iota(jnp.int32, (tiles, 128), 1) < bs

    def pair_rows(a, b):
        zero = jnp.zeros((tiles, 128), F32)
        a_even = zero if a is None else a
        b_even = zero if b is None else pltpu.roll(b, bs, 1)
        a_odd = zero if a is None else pltpu.roll(a, bs, 1)
        b_odd = zero if b is None else b
        return jnp.where(low_lane, a_even, b_even), jnp.where(low_lane, a_odd, b_odd)

    def unpack_chunk(c, carry):
        first = pl.multiple_of(c * CHUNK, CHUNK)
        for p in range(npair):
            x = lower[p, pl.ds(first, CHUNK), :].astype(F32)
            for t in range(tiles):
                spread[p, pl.ds(t * CHUNK, CHUNK), :] = x[:, t * 128 : (t + 1) * 128]
        lax.fori_loop(0, CHUNK // 2, functools.partial(unpack, c * CHUNK), 0)
        return carry

    def unpack(first, i, carry):
        for u in range(2):
            k = i * 2 + u
            s = first + k
            y = diag[s].astype(F32)
            for t in range(tiles):
                spread_d[u, pl.ds(t * 8, nblk), :] = y[:, t * 128 : (t + 1) * 128]
            for b in range(nblk):
                for jp in range(nblk // 2):
                    if 2 * jp < b:
                        parts = []
                        for j in (2 * jp, 2 * jp + 1):
                            if j < b:
                                slot = b * (b - 1) // 2 + j
                                rows = spread[slot, pl.ds(k, tiles, stride=CHUNK), :]
                                parts.append(rows * pattern[slot, s].astype(F32))
                            else:
                                parts.append(None)
                        even, odd = pair_rows(*parts)
                        wide[u, jp, pl.ds(b * bs, tiles, stride=2), :] = even
                        wide[u, jp, pl.ds(b * bs + 1, tiles, stride=2), :] = odd
                own = spread_d[u, pl.ds(b, tiles, stride=8), :]
                even, odd = pair_rows(*((own, None) if b % 2 == 0 else (None, own)))
                wide[u, nblk // 2, pl.ds(b * bs, tiles, stride=2), :] = even
                wide[u, nblk // 2, pl.ds(b * bs + 1, tiles, stride=2), :] = odd
            for jp in range(nblk // 2):
                lmat[s, :, pl.ds(jp * 128, 128)] = wide[u, jp].astype(BF16)
            dmat[s] = wide[u, nblk // 2].astype(BF16)
        return carry

    lax.fori_loop(0, subs // CHUNK, unpack_chunk, 0)

    for copy in loads[2:5]:
        copy.wait()

    @pl.when(me < last)
    def _():
        to_right.wait_send()
        to_left.wait_recv()

    @pl.when(me == last)
    def _():
        own_r.wait()

    @pl.when(me > 0)
    def _():
        to_left.wait_send()
        to_right.wait_recv()

    @pl.when(me == 0)
    def _():
        own_l.wait()

    base_l = jnp.maximum(me - 1, 0) * subs
    base_r = jnp.minimum(me + 1, last) * subs
    agg_base = me * n_agg

    def l1_part(g, u):
        low, high, off = window(width, u)
        first = pl.multiple_of(g * (UNROLL * width) + low, 128)
        return l1[:, pl.ds(first, high - low)], off

    def part_of(ref, a):
        low, high, off = window(width, a)
        return ref[:, pl.ds(low, high - low)], off

    def up(g, carry):
        ids = [g * UNROLL + u for u in range(UNROLL)]
        full = []
        for s in ids:
            mine = res[s]
            total = mine[:, inner:] + near(recv_l, neigh[0, s] - base_l) + near(recv_r, neigh[1, s] - base_r)
            full.append(jnp.concatenate([mine[:, :inner], total / 3.0], axis=1))
        for s, x in zip(ids, full):
            res[s] = x
        coarse = [mul_t(x, phi[s]) for s, x in zip(ids, full)]
        terms = [mul_part(x, *l1_part(g, u)) for u, x in enumerate(coarse)]
        for a in range(n_agg):
            acc = l2res[a]
            for s, x in zip(ids, terms):
                acc = acc + jnp.where(agg[s] - agg_base == a, 1.0, 0.0).astype(F32) * x
            l2res[a] = acc
        return carry

    lax.fori_loop(0, steps, up, 0)

    for copy in loads[5:]:
        copy.wait()

    def fine_step(g, carry):
        ids = [g * UNROLL + u for u in range(UNROLL)]
        base = [res[s] for s in ids]
        x = base
        for _ in range(nblk - 1):
            x = [b - mul_t(v, lmat[s]) for s, b, v in zip(ids, base, x)]
        mid = []
        for s, v in zip(ids, x):
            cols = [
                mul_t(v[:, jp * 128 : (jp + 1) * 128], dmat[s, pl.ds(jp * 128, 128), :])
                for jp in range(nblk // 2)
            ]
            mid.append(jnp.concatenate(cols, axis=1))
        x = mid
        for _ in range(nblk - 1):
            x = [b - mul(v, lmat[s]) for s, b, v in zip(ids, mid, x)]
        for s, v in zip(ids, x):
            fine[s] = v
        return carry

    def exchange(i, value):
        xsend[i] = value
        copy = pltpu.make_async_remote_copy(
            src_ref=xsend.at[i],
            dst_ref=xrecv.at[i],
            send_sem=x_send_sem.at[i],
            recv_sem=x_recv_sem.at[i],
            device_id=partners[i],
            device_id_type=MESH,
        )
        copy.start()
        return copy

    n_gap = len(partners) + 1
    cuts = [steps * i // n_gap for i in range(n_gap + 1)]

    def work(i):
        lax.fori_loop(cuts[i], cuts[i + 1], fine_step, 0)

    part = mul_part(l2res[0], *part_of(l2r, 0))
    for a in range(1, n_agg):
        part = part + mul_part(l2res[a], *part_of(l2r, a))
    copy = exchange(0, part)
    work(0)
    copy.wait()
    l3res = xsend[0] + xrecv[0]
    value = mul(l3res, l3r[...])
    for i in range(1, len(partners)):
        copy = exchange(i, value)
        work(i)
        copy.wait()
        value = xsend[i] + xrecv[i]
    group = dom // GROUP
    totals[group] = value
    sends = []
    for k in range(1, n_groups):
        copy = pltpu.make_async_remote_copy(
            src_ref=totals.at[group],
            dst_ref=totals.at[group],
            send_sem=t_send_sem.at[k - 1],
            recv_sem=t_recv_sem.at[k - 1],
            device_id=others[k - 1],
            device_id_type=MESH,
        )
        copy.start()
        sends.append(copy)
    work(n_gap - 1)
    for copy in sends:
        copy.wait()

    top_res = mul_part(totals[0], *part_of(l4r, 0))
    for p in range(1, n_groups):
        top_res = top_res + mul_part(totals[p], *part_of(l4r, p))
    top_corr = mul_t(top_res, top[...])
    two = pl.ds(pl.multiple_of(group // 2 * (2 * width), 128), 2 * width)
    l4two = mul(totals[group], l4i[:, two]) + mul(top_corr, l4r[:, two])
    l4corr = jnp.where(group % 2 == 0, l4two[:, :width], l4two[:, width:])
    l3corr = mul_t(xsend[0] + xrecv[0], l3i[...]) + mul_t(l4corr, l3r[...])
    for a in range(n_agg):
        l2corr[a] = mul_part_t(l2res[a], *part_of(l2i, a), width) + mul_part_t(
            l3corr, *part_of(l2r, a), width
        )

    def down(g, carry):
        ids = [g * UNROLL + u for u in range(UNROLL)]
        q = [near(l2corr, agg[s] - agg_base) for s in ids]
        coarse = [mul_part_t(x, *l1_part(g, u), width) for u, x in enumerate(q)]
        both = [mul(x, phi[s]) for s, x in zip(ids, coarse)]
        for s, x in zip(ids, both):
            fine[s] = fine[s] + x
        rows = pl.ds(g * UNROLL, UNROLL)
        pltpu.make_async_copy(fine.at[rows], out_h.at[rows], out_sem.at[g]).start()
        return carry

    lax.fori_loop(0, steps, down, 0)

    def drain(g, carry):
        rows = pl.ds(g * UNROLL, UNROLL)
        pltpu.make_async_copy(fine.at[rows], out_h.at[rows], out_sem.at[g]).wait()
        return carry

    lax.fori_loop(0, steps, drain, 0)


def solution(mesh):
    n_dom, n_lev = mesh.shape["dom"], mesh.shape["level"]

    def per_device(
        residual,
        neighbours,
        pattern,
        diag_inverse,
        lower_blocks,
        phi,
        aggregate,
        level1_restrict,
        level2_interior_solve,
        level2_restrict,
        level3_interior_solve,
        level3_restrict,
        level4_interior_solve,
        level4_restrict,
        top_inverse,
    ):
        subs, rhs, dofs = residual.shape
        width = top_inverse.shape[0]
        nblk = diag_inverse.shape[1]
        edge = 2 * (dofs // nblk)
        tiles = lower_blocks.shape[2] // 128
        n_agg = subs // 8
        n_groups = n_dom // GROUP
        n_x = 4
        lower_t = lower_blocks.transpose(1, 0, 2)
        large = [
            residual,
            diag_inverse,
            lower_t,
            phi,
            level1_restrict.T,
            level2_interior_solve.T,
            level2_restrict.T,
            level3_interior_solve,
            level3_restrict,
            level4_interior_solve.T,
            level4_restrict.T,
            top_inverse,
        ]
        scratch = [pltpu.VMEM(a.shape, a.dtype) for a in large]
        scratch += [
            pltpu.VMEM((subs, rhs, edge), F32),
            pltpu.VMEM((subs, rhs, edge), F32),
            pltpu.VMEM((lower_t.shape[0], tiles * CHUNK, 128), F32),
            pltpu.VMEM((2, tiles * 8, 128), F32),
            pltpu.VMEM((2, nblk // 2 + 1, dofs, 128), F32),
            pltpu.VMEM((subs, dofs, dofs), BF16),
            pltpu.VMEM((subs, dofs, 128), BF16),
            pltpu.VMEM((subs, rhs, dofs), F32),
            pltpu.VMEM((n_agg, rhs, width), F32),
            pltpu.VMEM((n_agg, rhs, width), F32),
            pltpu.VMEM((n_x, rhs, width), F32),
            pltpu.VMEM((n_x, rhs, width), F32),
            pltpu.VMEM((n_groups, rhs, width), F32),
            pltpu.SemaphoreType.DMA((len(large),)),
            pltpu.SemaphoreType.DMA((2,)),
            pltpu.SemaphoreType.DMA((2,)),
            pltpu.SemaphoreType.DMA((2,)),
            pltpu.SemaphoreType.DMA((n_x,)),
            pltpu.SemaphoreType.DMA((n_x,)),
            pltpu.SemaphoreType.DMA((max(n_groups - 1, 1),)),
            pltpu.SemaphoreType.DMA((max(n_groups - 1, 1),)),
            pltpu.SemaphoreType.DMA((subs // UNROLL,)),
        ]
        return pl.pallas_call(
            functools.partial(kernel, n_dom, n_lev),
            out_shape=jax.ShapeDtypeStruct(residual.shape, F32),
            in_specs=[pl.BlockSpec(memory_space=pltpu.SMEM)] * 3
            + [pl.BlockSpec(memory_space=pl.ANY)] * len(large),
            out_specs=pl.BlockSpec(memory_space=pl.ANY),
            scratch_shapes=scratch,
            compiler_params=pltpu.CompilerParams(
                collective_id=0, has_side_effects=True, vmem_limit_bytes=56 * 2**20
            ),
            cost_estimate=pl.CostEstimate(
                flops=10**9, bytes_accessed=13 * 10**6, transcendentals=0
            ),
        )(neighbours.T, pattern.T, aggregate, *large)

    both = P(("dom", "level"))
    in_specs = (both,) * 10 + (P("dom"),) * 2 + (P(),) * 3
    return jax.shard_map(
        per_device, mesh=mesh, in_specs=in_specs, out_specs=both, check_vma=False
    )
```
